32 devices in a mesh: groups: 2 (over y), lat: 8 (over z, x), tp: 2 (over core).
Axes of the slice: x: 2, y: 2, z: 4, core: 2. Of those that a mesh axis runs over, the one named last changes fastest.
Arguments:
- partials: bfloat16 [2, 128, 4608], P('tp', ('groups', 'lat')), parts along dimension 1, may hold values from -5 to 5
- token_ids: int32 [128], P('groups'), parts along dimension 0, may hold values from 0 to 255999, as said below
- enc_weight: bfloat16 [3072, 4608], P('lat'), may hold values from -0.09375 to 0.09375
- enc_bias: float32 [3072], P('lat'), may hold values from -3 to 3
- dec_weight: bfloat16 [3072, 4608], P('lat'), may hold values from -0.109375 to 0.109375
Outputs:
- recon: bfloat16 [128, 4608], P(('groups', 'lat', 'tp')), parts along dimension 0
- input_grad: float32 [128, 4608], P(('groups', 'lat', 'tp')), parts along dimension 0
- grad_enc: bfloat16 [6144, 4608], P(('groups', 'lat', 'tp')), parts along dimension 0
- grad_dec: bfloat16 [6144, 4608], P(('groups', 'lat', 'tp')), parts along dimension 0
- grad_bias: float32 [6144], P(('groups', 'lat', 'tp')), parts along dimension 0
The draws below stay inside these ranges and needn't reach their ends.
There are 2 independent parts, one for each index of `groups`. The reference program is written for one: setup_inputs(seed, part) draws one part's arguments, and reference() takes and returns one part's arrays. A program takes and returns all parts, laid end to end along the dimension named above; an argument that names none is the same for every part. Nothing has to cross between parts.
Inputs may be any that keep to these rules, and one draw needn't show every extreme that they name: `token_ids`: ids 0, 1 and 2 are padding, end and beginning markers; the others are ordinary tokens.
All inputs are finite; a program needn't handle non-finite values.
Results may differ from the reference program's by a relative error of at most 0.009.
Values may be sent and summed in bfloat16 or wider, within the bound.
A program may use at most 128 MiB of HBM per device.

```python
import jax
import jax.numpy as jnp
from jax import lax

D = 4608
VOCAB = 256000
SHARDS = 2
TOKENS = 64
LATENTS = 3072


def draw_token_ids(key, part):
    key = jax.random.fold_in(key, 11)
    first, second, third = jax.random.split(key, 3)
    marker = jax.random.randint(first, (TOKENS,), 0, 8) == 0
    lowid = jax.random.randint(second, (TOKENS,), 0, 3)
    highid = jax.random.randint(third, (TOKENS,), 3, VOCAB)
    return jnp.where(marker, lowid, highid).astype(jnp.int32)


def block_levels(stream_key, dims, shards, least, top_value):
    gain, own = 1.0, jax.random.fold_in(stream_key, 6)
    for dim, shards_of in shards:
        heights = jnp.exp(jax.random.uniform(jax.random.fold_in(own, dim), (shards_of,), jnp.float32, least / len(shards), top_value / len(shards)))
        gain = gain * jnp.repeat(heights, dims[dim] // shards_of).reshape([-1 if axis == dim else 1 for axis in range(len(dims))])
    return gain


def normal_values(key, dims, deviation, reach, cuts=(), held_as=jnp.bfloat16):
    drawn = jax.random.normal(key, dims, jnp.float32) * deviation
    if len(cuts) > 0:
        drawn = block_levels(key, dims, cuts, -0.22, 0.18) * drawn
    return jnp.clip(drawn, min=-reach, max=reach).astype(held_as)


def setup_inputs(seed: int = 0, part: int = 0) -> dict:
    streams_of = jax.random.split(jax.random.key(seed), 6)
    part_keys = jax.random.split(jax.random.fold_in(streams_of[5], part), 6)
    partials = normal_values(part_keys[0], (SHARDS, TOKENS, D), 0.7, 5.0, ((0, 2), (1, 8)))
    token_ids = draw_token_ids(jax.random.fold_in(jax.random.fold_in(streams_of[5], part), 71), part)
    enc_weight = normal_values(streams_of[2], (LATENTS, D), D ** -0.5, 0.09375, ((0, 8),))
    enc_bias = normal_values(streams_of[3], (LATENTS,), 0.5, 3.0, ((0, 8),), jnp.float32)
    dec_weight = normal_values(streams_of[4], (LATENTS, D), LATENTS ** -0.5, 0.109375, ((0, 8),))
    return dict(partials=partials, token_ids=token_ids, enc_weight=enc_weight, enc_bias=enc_bias, dec_weight=dec_weight)


l1_weight = 0.2


def reference(partials, token_ids, enc_weight, enc_bias, dec_weight):
    acts = jnp.sum(partials.astype(jnp.float32), axis=0).astype(jnp.bfloat16)
    keep = (token_ids >= 3).astype(jnp.float32)[:, None]
    pre = lax.dot_general(acts, enc_weight, (((1,), (1,)), ((), ())), preferred_element_type=jnp.float32) + enc_bias
    act = (jax.nn.softplus(8.0 * pre) / 8.0).astype(jnp.bfloat16)
    slope = jax.nn.sigmoid(8.0 * pre)
    total = jnp.dot(act, dec_weight, preferred_element_type=jnp.float32)
    recon = total.astype(jnp.bfloat16)
    signal = (keep * (total - acts.astype(jnp.float32))).astype(jnp.bfloat16)
    back = lax.dot_general(signal, dec_weight, (((1,), (1,)), ((), ())), preferred_element_type=jnp.float32) + l1_weight * keep
    dpre = (back * slope).astype(jnp.bfloat16)
    grad_enc = lax.dot_general(dpre, acts, (((0,), (0,)), ((), ())), preferred_element_type=jnp.float32).astype(jnp.bfloat16)
    grad_dec = lax.dot_general(act, signal, (((0,), (0,)), ((), ())), preferred_element_type=jnp.float32).astype(jnp.bfloat16)
    grad_bias = jnp.sum(dpre.astype(jnp.float32), axis=0)
    input_grad = jnp.dot(dpre, enc_weight, preferred_element_type=jnp.float32) - signal.astype(jnp.float32)
    return recon, input_grad, grad_enc, grad_dec, grad_bias
```

```python
import functools

import jax
import jax.numpy as jnp
from jax import lax
from jax.experimental import pallas as pl
from jax.experimental.pallas import tpu as pltpu
from jax.sharding import PartitionSpec as P

L1_WEIGHT = 0.2
f32, bf16 = jnp.float32, jnp.bfloat16
NEAR = 2


def kernel(
    far, tokens, lats, width,
    part_ref, ids_ref, enc_hbm, bias_ref, dec_hbm,
    recon_ref, igrad_ref, genc_hbm, gdec_hbm, gbias_ref,
    enc, dec, genc, gdec,
    part, part_in, acts_all, signal_all, acts, signal,
    outgoing, pair_in, near_out, near_in, far_out, far_in, swap, swap_wide,
    load_sem, store_sem, pair_sems, ag_far, ag_near, ag_core, rs_core, rs_near, rs_far, swap_sems,
):
    quarter = width // 4
    half = width // 2
    lat = lax.axis_index("lat")
    core = lax.axis_index("tp")
    other = 1 - core
    a, b = lat // NEAR, lat % NEAR
    nb = 1 - b

    def fars(k, sign):
        return lax.rem(a + sign * k + far, far)

    def send(src, dst, sems, index, to_lat, to_core):
        copy = pltpu.make_async_remote_copy(
            src_ref=src,
            dst_ref=dst,
            send_sem=sems.at[(0, *index)],
            recv_sem=sems.at[(1, *index)],
            device_id={"lat": to_lat, "tp": to_core},
            device_id_type=pl.DeviceIdType.MESH,
        )
        copy.start()
        return copy

    loads = []
    for i, (hbm, vmem) in enumerate(((enc_hbm, enc), (dec_hbm, dec))):
        copy = pltpu.make_async_copy(
            hbm.at[pl.ds(pl.multiple_of(core * lats, lats), lats), :], vmem, load_sem.at[i]
        )
        copy.start()
        loads.append(copy)

    barrier = pltpu.get_barrier_semaphore()
    peers = [(lat, other), (a * NEAR + nb, core)]
    peers += [(fars(k, 1) * NEAR + b, core) for k in range(1, far)]
    for to_lat, to_core in peers:
        pl.semaphore_signal(
            barrier, inc=1, device_id={"lat": to_lat, "tp": to_core},
            device_id_type=pl.DeviceIdType.MESH,
        )

    mine = part_ref[0].astype(f32)
    for h in range(2):
        part[h] = jnp.concatenate(
            [mine[:, h * half:h * half + quarter], mine[:, h * half + quarter:(h + 1) * half]], axis=0
        ).astype(bf16)

    keep_row = (ids_ref[...] >= 3).astype(f32)

    def keep_column(rows, token_of):
        at = lax.broadcasted_iota(jnp.int32, (rows, tokens), 1)
        row = lax.broadcasted_iota(jnp.int32, (rows, tokens), 0)
        return jnp.sum(jnp.where(at == token_of(row), keep_row, 0.0), axis=1, keepdims=True)

    keep = keep_column(tokens, lambda i: (((i // 8) % far) * NEAR + (i // 8) // far) * 8 + i % 8)
    keep_mine = keep_column(16, lambda i: lat * 8 + i % 8)

    pl.semaphore_wait(barrier, len(peers))

    def gather(turn, ref, beside=None):
        mine_at = ref.at[core, b, a]
        sent = [
            send(mine_at, mine_at, ag_far, (turn, k), fars(k, 1) * NEAR + b, core)
            for k in range(1, far)
        ]
        near_copies, core_copies = [], []
        for k in range(far):
            origin = fars(k, -1)
            if k > 0:
                sent[k - 1].wait_recv()
            block = ref.at[core, b, origin]
            near_copies.append(send(block, block, ag_near, (turn, k), a * NEAR + nb, core))
            core_copies.append(send(block, block, ag_core, (turn, k), lat, other))
        if beside is not None:
            beside()
        for k in range(far):
            near_copies[k].wait_recv()
            block = ref.at[core, nb, fars(k, -1)]
            core_copies.append(send(block, block, ag_core, (turn, far + k), lat, other))
        for copy in core_copies:
            copy.wait_recv()
        for copy in sent + near_copies + core_copies:
            copy.wait_send()

    def unpack(ref, out):
        for h in range(2):
            blocks = ref[h].astype(f32).reshape(NEAR * far, 16, quarter)
            for s in range(2):
                out[2 * h + s] = (
                    blocks[:, 8 * s:8 * s + 8, :].reshape(tokens, quarter).astype(bf16)
                )

    def contribution(left, weight, h):
        pieces = []
        for s in range(2):
            columns = pl.ds(pl.multiple_of(h * half + s * quarter, 128), quarter)
            piece = jnp.dot(left, weight[:, columns], preferred_element_type=f32)
            pieces.append(piece.reshape(NEAR, far, 8, quarter))
        outgoing[h] = jnp.concatenate(pieces, axis=2).astype(bf16)

    def scatter(turn, left, weight, beside):
        contribution(left, weight, other)
        first = [
            send(outgoing.at[other, side], pair_in.at[turn, side], rs_core, (turn, i), lat, other)
            for i, side in enumerate((nb, b))
        ]
        contribution(left, weight, core)
        first[0].wait_recv()
        near_copies = []
        for k in [*range(1, far), 0]:
            to = fars(k, 1)
            near_out[to] = (
                outgoing[core, nb, to].astype(f32) + pair_in[turn, nb, to].astype(f32)
            ).astype(bf16)
            near_copies.append(
                send(near_out.at[to], near_in.at[turn, to], rs_near, (turn, k), a * NEAR + nb, core)
            )
        beside[0]()
        first[1].wait_recv()
        far_copies = []
        for k in [*range(1, far), 0]:
            to = fars(k, 1)
            near_copies[k - 1 if k > 0 else far - 1].wait_recv()
            summed = (
                outgoing[core, b, to].astype(f32)
                + pair_in[turn, b, to].astype(f32)
                + near_in[turn, to].astype(f32)
            )
            if k > 0:
                far_out[k] = summed.astype(bf16)
                far_copies.append(
                    send(far_out.at[k], far_in.at[turn, k], rs_far, (turn, k), to * NEAR + b, core)
                )
        beside[1]()
        for k in range(1, far):
            far_copies[k - 1].wait_recv()
            summed = summed + far_in[turn, k].astype(f32)
        for copy in first + near_copies + far_copies:
            copy.wait_send()
        return summed

    pair = send(part.at[other], part_in, pair_sems, (), lat, other)
    pair.wait_recv()
    acts_all[core, b, a] = (part[core].astype(f32) + part_in[...].astype(f32)).astype(bf16)
    gather(0, acts_all, loads[0].wait)
    pair.wait_send()
    unpack(acts_all, acts)

    def against(matrix, weight):
        total = None
        for q in range(4):
            term = lax.dot_general(
                matrix[q], weight[:, q * quarter:(q + 1) * quarter],
                (((1,), (1,)), ((), ())), preferred_element_type=f32,
            )
            total = term if total is None else total + term
        return total

    bias = jnp.where(core == 0, bias_ref[:, :lats], bias_ref[:, lats:])
    eight = 8.0 * (against(acts, enc) + bias)
    small = jnp.exp(-jnp.abs(eight))
    act = ((jnp.maximum(eight, 0.0) + jnp.log1p(small)) / 8.0).astype(bf16)
    slope = jnp.where(eight >= 0, 1.0, small) / (1.0 + small)

    def nothing():
        pass

    loads[1].wait()
    total = scatter(0, act, dec, (nothing, nothing))
    signal_mine = (keep_mine * (total - acts_all[core, b, a].astype(f32))).astype(bf16)
    signal_all[core, b, a] = signal_mine

    recon_copies = []

    def send_recon():
        swap[core] = total.astype(bf16)
        recon_copies.append(send(swap.at[core], swap.at[core], swap_sems, (0,), lat, other))

    gather(1, signal_all, send_recon)
    unpack(signal_all, signal)

    back = against(signal, dec) + L1_WEIGHT * keep
    dpre = (back * slope).astype(bf16)
    stores = []

    def gradient(left, matrix, vmem, hbm, index):
        for q in range(4):
            columns = slice(q * quarter, (q + 1) * quarter)
            vmem[:, columns] = lax.dot_general(
                left, matrix[q], (((0,), (0,)), ((), ())), preferred_element_type=f32
            ).astype(bf16)
        copy = pltpu.make_async_copy(vmem, hbm, store_sem.at[index])
        copy.start()
        stores.append(copy)

    def enc_side():
        gradient(dpre, acts, genc, genc_hbm, 0)

    def own_rows(pair):
        for h in range(2):
            for s in range(2):
                block = pair[h][8 * s:8 * s + 8].astype(f32)
                yield (2 * h + s) * quarter, jnp.where(core == 0, block[:4], block[4:])

    def dec_side():
        gradient(act, signal, gdec, gdec_hbm, 1)
        gbias_ref[...] = jnp.sum(dpre.astype(f32), axis=0, keepdims=True)
        recon_copies[0].wait_recv()
        for at, rows in own_rows(swap):
            recon_ref[:, at:at + quarter] = rows.astype(bf16)

    inward = scatter(1, dpre, enc, (enc_side, dec_side))
    swap_wide[core] = inward - signal_mine.astype(f32)
    last = send(swap_wide.at[core], swap_wide.at[core], swap_sems, (1,), lat, other)
    last.wait_recv()
    for at, rows in own_rows(swap_wide):
        igrad_ref[:, at:at + quarter] = rows
    last.wait_send()
    recon_copies[0].wait_send()
    for copy in stores:
        copy.wait()


def on_device(partials, token_ids, enc_weight, enc_bias, dec_weight):
    n_lat = lax.axis_size("lat")
    far = n_lat // NEAR
    tokens = token_ids.shape[0]
    width = enc_weight.shape[1]
    lats = enc_weight.shape[0] // 2
    quarter = width // 4
    vmem = pl.BlockSpec(memory_space=pltpu.VMEM)
    hbm = pl.BlockSpec(memory_space=pl.ANY)
    dma = pltpu.SemaphoreType.DMA
    flops = 2 * 6 * tokens * lats * width
    recon, igrad, genc, gdec, gbias = pl.pallas_call(
        functools.partial(kernel, far, tokens, lats, width),
        out_shape=(
            jax.ShapeDtypeStruct((4, width), bf16),
            jax.ShapeDtypeStruct((4, width), f32),
            jax.ShapeDtypeStruct((lats, width), bf16),
            jax.ShapeDtypeStruct((lats, width), bf16),
            jax.ShapeDtypeStruct((1, lats), f32),
        ),
        in_specs=[vmem, vmem, hbm, vmem, hbm],
        out_specs=(vmem, vmem, hbm, hbm, vmem),
        scratch_shapes=[
            pltpu.VMEM((lats, width), bf16),
            pltpu.VMEM((lats, width), bf16),
            pltpu.VMEM((lats, width), bf16),
            pltpu.VMEM((lats, width), bf16),
            pltpu.VMEM((2, 16, quarter), bf16),
            pltpu.VMEM((16, quarter), bf16),
            pltpu.VMEM((2, NEAR, far, 16, quarter), bf16),
            pltpu.VMEM((2, NEAR, far, 16, quarter), bf16),
            pltpu.VMEM((4, tokens, quarter), bf16),
            pltpu.VMEM((4, tokens, quarter), bf16),
            pltpu.VMEM((2, NEAR, far, 16, quarter), bf16),
            pltpu.VMEM((2, NEAR, far, 16, quarter), bf16),
            pltpu.VMEM((far, 16, quarter), bf16),
            pltpu.VMEM((2, far, 16, quarter), bf16),
            pltpu.VMEM((far, 16, quarter), bf16),
            pltpu.VMEM((2, far, 16, quarter), bf16),
            pltpu.VMEM((2, 16, quarter), bf16),
            pltpu.VMEM((2, 16, quarter), f32),
            dma((2,)),
            dma((2,)),
            dma((2,)),
            dma((2, 2, far)),
            dma((2, 2, far)),
            dma((2, 2, 2 * far)),
            dma((2, 2, 2)),
            dma((2, 2, far)),
            dma((2, 2, far)),
            dma((2, 2)),
        ],
        compiler_params=pltpu.CompilerParams(
            collective_id=0, has_side_effects=True, vmem_limit_bytes=60 * 2**20
        ),
        cost_estimate=pl.CostEstimate(
            flops=flops, bytes_accessed=8 * lats * width, transcendentals=4 * tokens * lats
        ),
    )(partials, token_ids.reshape(1, -1), enc_weight, enc_bias.reshape(1, -1), dec_weight)
    return recon, igrad, genc, gdec, gbias.reshape(-1)


def solution(mesh):
    placed = (
        P("tp", ("groups", "lat"), None),
        P("groups"),
        P("lat", None),
        P("lat"),
        P("lat", None),
    )
    split = P(("groups", "lat", "tp"), None)
    return jax.shard_map(
        on_device,
        mesh=mesh,
        in_specs=placed,
        out_specs=(split, split, split, split, P(("groups", "lat", "tp"))),
        check_vma=False,
    )
```

```python
import functools

import jax
import jax.numpy as jnp
from jax import lax
from jax.experimental import pallas as pl
from jax.experimental.pallas import tpu as pltpu
from jax.sharding import PartitionSpec as P

L1_WEIGHT = 0.2
f32, bf16 = jnp.float32, jnp.bfloat16
NEAR = 2


def kernel(
    far, tokens, lats, width,
    part_ref, ids_ref, enc_hbm, bias_ref, dec_hbm,
    recon_ref, igrad_ref, genc_hbm, gdec_hbm, gbias_ref,
    enc, dec, genc, gdec,
    part, part_in, acts_all, signal_all, acts, signal,
    outgoing, plane_in, far_out, far_in,
    load_sem, store_sem, pair_sems, ag_far, ag_plane, rs_plane, rs_far,
):
    quarter = width // 4
    lat = lax.axis_index("lat")
    core = lax.axis_index("tp")
    other = 1 - core
    a, b = lat // NEAR, lat % NEAR
    nb = 1 - b

    def fars(k, sign):
        return lax.rem(a + sign * k + far, far)

    def send(src, dst, sems, index, to_lat, to_core):
        copy = pltpu.make_async_remote_copy(
            src_ref=src,
            dst_ref=dst,
            send_sem=sems.at[(0, *index)],
            recv_sem=sems.at[(1, *index)],
            device_id={"lat": to_lat, "tp": to_core},
            device_id_type=pl.DeviceIdType.MESH,
        )
        copy.start()
        return copy

    loads = []
    for i, (hbm, vmem) in enumerate(((enc_hbm, enc), (dec_hbm, dec))):
        copy = pltpu.make_async_copy(
            hbm.at[pl.ds(pl.multiple_of(core * lats, lats), lats), :], vmem, load_sem.at[i]
        )
        copy.start()
        loads.append(copy)

    barrier = pltpu.get_barrier_semaphore()
    plane = [(nb, core), (nb, other), (b, other)]
    peers = [(a * NEAR + near, k) for near, k in plane]
    peers += [(fars(k, 1) * NEAR + b, core) for k in range(1, far)]
    for to_lat, to_core in peers:
        pl.semaphore_signal(
            barrier, inc=1, device_id={"lat": to_lat, "tp": to_core},
            device_id_type=pl.DeviceIdType.MESH,
        )

    mine = part_ref[0].astype(f32)
    quarters = [mine[:, q * quarter:(q + 1) * quarter] for q in range(4)]
    for k in range(2):
        part[k] = jnp.concatenate([v[4 * k:4 * k + 4] for v in quarters], axis=0).astype(bf16)

    keep_row = (ids_ref[...] >= 3).astype(f32)

    def keep_column(rows, token_of):
        at = lax.broadcasted_iota(jnp.int32, (rows, tokens), 1)
        row = lax.broadcasted_iota(jnp.int32, (rows, tokens), 0)
        return jnp.sum(jnp.where(at == token_of(row), keep_row, 0.0), axis=1, keepdims=True)

    keep = keep_column(tokens, lambda i: (((i // 8) % far) * NEAR + (i // 8) // far) * 8 + i % 8)
    keep_mine = keep_column(16, lambda i: lat * 8 + core * 4 + i % 4)

    pl.semaphore_wait(barrier, len(peers))

    def gather(turn, ref, beside=None):
        mine_at = ref.at[core, b, a]
        sent = [
            send(mine_at, mine_at, ag_far, (turn, k), fars(k, 1) * NEAR + b, core)
            for k in range(1, far)
        ]
        passed = []
        for k in range(far):
            if k > 0:
                sent[k - 1].wait_recv()
            block = ref.at[core, b, fars(k, -1)]
            for slot, (near, to_core) in enumerate(plane):
                passed.append(
                    send(block, block, ag_plane, (turn, slot, k), a * NEAR + near, to_core)
                )
            if k == 0 and beside is not None:
                beside()
        for copy in passed:
            copy.wait_recv()
        for copy in sent + passed:
            copy.wait_send()

    def unpack(ref, out):
        halves = [ref[k].astype(f32).reshape(NEAR * far, 16, quarter) for k in range(2)]
        for q in range(4):
            out[q] = (
                jnp.concatenate([v[:, 4 * q:4 * q + 4, :] for v in halves], axis=1)
                .reshape(tokens, quarter)
                .astype(bf16)
            )

    def scatter(turn, left, weight, beside):
        pieces = [
            jnp.dot(
                left, weight[:, q * quarter:(q + 1) * quarter], preferred_element_type=f32
            ).reshape(NEAR * far, 8, quarter)
            for q in range(4)
        ]
        for k in range(2):
            rows = jnp.concatenate([v[:, 4 * k:4 * k + 4, :] for v in pieces], axis=1)
            outgoing[k] = rows.astype(bf16).reshape(NEAR, far, 16, quarter)
        order = [*range(1, far), 0]
        first = {}
        for k in order:
            to = fars(k, 1)
            for slot, (near, to_core) in enumerate(plane):
                first[slot, k] = send(
                    outgoing.at[to_core, near, to], plane_in.at[turn, slot, to],
                    rs_plane, (turn, slot, k), a * NEAR + near, to_core,
                )
        beside[0]()
        far_copies = []
        for k in order:
            to = fars(k, 1)
            summed = outgoing[core, b, to].astype(f32)
            for slot in range(3):
                first[slot, k].wait_recv()
                summed = summed + plane_in[turn, slot, to].astype(f32)
            if k > 0:
                far_out[k] = summed.astype(bf16)
                far_copies.append(
                    send(far_out.at[k], far_in.at[turn, k], rs_far, (turn, k), to * NEAR + b, core)
                )
        beside[1]()
        for k in range(1, far):
            far_copies[k - 1].wait_recv()
            summed = summed + far_in[turn, k].astype(f32)
        for copy in [*first.values(), *far_copies]:
            copy.wait_send()
        return summed

    pair = send(part.at[other], part_in, pair_sems, (), lat, other)
    pair.wait_recv()
    acts_all[core, b, a] = (part[core].astype(f32) + part_in[...].astype(f32)).astype(bf16)
    gather(0, acts_all, loads[0].wait)
    pair.wait_send()
    unpack(acts_all, acts)

    def against(matrix, weight):
        total = None
        for q in range(4):
            term = lax.dot_general(
                matrix[q], weight[:, q * quarter:(q + 1) * quarter],
                (((1,), (1,)), ((), ())), preferred_element_type=f32,
            )
            total = term if total is None else total + term
        return total

    bias = jnp.where(core == 0, bias_ref[:, :lats], bias_ref[:, lats:])
    eight = 8.0 * (against(acts, enc) + bias)
    small = jnp.exp(-jnp.abs(eight))
    act = ((jnp.maximum(eight, 0.0) + jnp.log1p(small)) / 8.0).astype(bf16)
    slope = jnp.where(eight >= 0, 1.0, small) / (1.0 + small)

    def nothing():
        pass

    loads[1].wait()
    total = scatter(0, act, dec, (nothing, nothing))
    signal_mine = (keep_mine * (total - acts_all[core, b, a].astype(f32))).astype(bf16)
    signal_all[core, b, a] = signal_mine

    def write_recon():
        for q in range(4):
            recon_ref[:, q * quarter:(q + 1) * quarter] = total[4 * q:4 * q + 4].astype(bf16)

    gather(1, signal_all, write_recon)
    unpack(signal_all, signal)

    back = against(signal, dec) + L1_WEIGHT * keep
    dpre = (back * slope).astype(bf16)
    stores = []

    def gradient(left, matrix, vmem, hbm, index):
        for q in range(4):
            columns = slice(q * quarter, (q + 1) * quarter)
            vmem[:, columns] = lax.dot_general(
                left, matrix[q], (((0,), (0,)), ((), ())), preferred_element_type=f32
            ).astype(bf16)
        copy = pltpu.make_async_copy(vmem, hbm, store_sem.at[index])
        copy.start()
        stores.append(copy)

    def enc_side():
        gradient(dpre, acts, genc, genc_hbm, 0)

    def dec_side():
        gradient(act, signal, gdec, gdec_hbm, 1)
        gbias_ref[...] = jnp.sum(dpre.astype(f32), axis=0, keepdims=True)

    inward = scatter(1, dpre, enc, (enc_side, dec_side))
    inward = inward - signal_mine.astype(f32)
    for q in range(4):
        igrad_ref[:, q * quarter:(q + 1) * quarter] = inward[4 * q:4 * q + 4]
    for copy in stores:
        copy.wait()


def deliver(
    parts, recon_in, igrad_in, genc_in, gdec_in, gbias_in, recon, igrad, genc, gdec, gbias, sems
):
    copies = []
    for source, target in ((genc_in, genc), (gdec_in, gdec)):
        rows = source.shape[0] // parts
        for i in range(parts):
            at = pl.ds(i * rows, rows)
            copies.append((source.at[at, :], target.at[at, :]))
    copies += [(recon_in, recon), (igrad_in, igrad), (gbias_in, gbias)]
    started = []
    for i, (source, target) in enumerate(copies):
        copy = pltpu.make_async_copy(source, target, sems.at[i])
        copy.start()
        started.append(copy)
    for copy in started:
        copy.wait()


def on_device(partials, token_ids, enc_weight, enc_bias, dec_weight):
    n_lat = lax.axis_size("lat")
    far = n_lat // NEAR
    tokens = token_ids.shape[0]
    width = enc_weight.shape[1]
    lats = enc_weight.shape[0] // 2
    quarter = width // 4
    vmem = pl.BlockSpec(memory_space=pltpu.VMEM)
    hbm = pl.BlockSpec(memory_space=pl.ANY)
    dma = pltpu.SemaphoreType.DMA
    flops = 2 * 6 * tokens * lats * width
    recon, igrad, genc, gdec, gbias = pl.pallas_call(
        functools.partial(kernel, far, tokens, lats, width),
        out_shape=(
            jax.ShapeDtypeStruct((4, width), bf16),
            jax.ShapeDtypeStruct((4, width), f32),
            jax.ShapeDtypeStruct((lats, width), bf16),
            jax.ShapeDtypeStruct((lats, width), bf16),
            jax.ShapeDtypeStruct((1, lats), f32),
        ),
        in_specs=[vmem, vmem, hbm, vmem, hbm],
        out_specs=(vmem, vmem, hbm, hbm, vmem),
        scratch_shapes=[
            pltpu.VMEM((lats, width), bf16),
            pltpu.VMEM((lats, width), bf16),
            pltpu.VMEM((lats, width), bf16),
            pltpu.VMEM((lats, width), bf16),
            pltpu.VMEM((2, 16, quarter), bf16),
            pltpu.VMEM((16, quarter), bf16),
            pltpu.VMEM((2, NEAR, far, 16, quarter), bf16),
            pltpu.VMEM((2, NEAR, far, 16, quarter), bf16),
            pltpu.VMEM((4, tokens, quarter), bf16),
            pltpu.VMEM((4, tokens, quarter), bf16),
            pltpu.VMEM((2, NEAR, far, 16, quarter), bf16),
            pltpu.VMEM((2, 3, far, 16, quarter), bf16),
            pltpu.VMEM((far, 16, quarter), bf16),
            pltpu.VMEM((2, far, 16, quarter), bf16),
            dma((2,)),
            dma((2,)),
            dma((2,)),
            dma((2, 2, far)),
            dma((2, 2, 3, far)),
            dma((2, 2, 3, far)),
            dma((2, 2, far)),
        ],
        compiler_params=pltpu.CompilerParams(
            collective_id=0, has_side_effects=True, vmem_limit_bytes=60 * 2**20
        ),
        cost_estimate=pl.CostEstimate(
            flops=flops, bytes_accessed=8 * lats * width, transcendentals=4 * tokens * lats
        ),
    )(partials, token_ids.reshape(1, -1), enc_weight, enc_bias.reshape(1, -1), dec_weight)
    made = (recon, igrad, genc, gdec, gbias)
    recon, igrad, genc, gdec, gbias = pl.pallas_call(
        functools.partial(deliver, 4),
        out_shape=tuple(jax.ShapeDtypeStruct(x.shape, x.dtype) for x in made),
        in_specs=[hbm] * 5,
        out_specs=(hbm,) * 5,
        scratch_shapes=[dma((11,))],
        compiler_params=pltpu.CompilerParams(vmem_limit_bytes=60 * 2**20),
        cost_estimate=pl.CostEstimate(
            flops=0, bytes_accessed=8 * lats * width, transcendentals=0
        ),
    )(*made)
    return recon, igrad, genc, gdec, gbias.reshape(-1)


def solution(mesh):
    placed = (
        P("tp", ("groups", "lat"), None),
        P("groups"),
        P("lat", None),
        P("lat"),
        P("lat", None),
    )
    split = P(("groups", "lat", "tp"), None)
    return jax.shard_map(
        on_device,
        mesh=mesh,
        in_specs=placed,
        out_specs=(split, split, split, split, P(("groups", "lat", "tp"))),
        check_vma=False,
    )
```

```python
import functools

import jax
import jax.numpy as jnp
from jax import lax
from jax.experimental import pallas as pl
from jax.experimental.pallas import tpu as pltpu
from jax.sharding import PartitionSpec as P

L1_WEIGHT = 0.2
f32, bf16 = jnp.float32, jnp.bfloat16
NEAR = 2


def kernel(
    far, tokens, lats, width,
    part_ref, ids_ref, enc_hbm, bias_ref, dec_hbm,
    recon_ref, igrad_ref, acts_hbm, signal_hbm, act_ref, dpre_ref,
    enc, dec,
    part, part_in, acts_all, signal_all, acts, signal,
    outgoing, pair_in, near_out, near_in, far_out, far_in,
    load_sem, store_sem, pair_sems, ag_far, ag_near, ag_core, rs_core, rs_near, rs_far,
):
    quarter = width // 4
    lat = lax.axis_index("lat")
    core = lax.axis_index("tp")
    other = 1 - core
    a, b = lat // NEAR, lat % NEAR
    nb = 1 - b

    def fars(k, sign):
        return lax.rem(a + sign * k + far, far)

    def send(src, dst, sems, index, to_lat, to_core):
        copy = pltpu.make_async_remote_copy(
            src_ref=src,
            dst_ref=dst,
            send_sem=sems.at[(0, *index)],
            recv_sem=sems.at[(1, *index)],
            device_id={"lat": to_lat, "tp": to_core},
            device_id_type=pl.DeviceIdType.MESH,
        )
        copy.start()
        return copy

    loads = []
    for i, (hbm, vmem) in enumerate(((enc_hbm, enc), (dec_hbm, dec))):
        copy = pltpu.make_async_copy(
            hbm.at[pl.ds(pl.multiple_of(core * lats, lats), lats), :], vmem, load_sem.at[i]
        )
        copy.start()
        loads.append(copy)

    barrier = pltpu.get_barrier_semaphore()
    peers = [(lat, other), (a * NEAR + nb, core)]
    peers += [(fars(k, 1) * NEAR + b, core) for k in range(1, far)]
    for to_lat, to_core in peers:
        pl.semaphore_signal(
            barrier, inc=1, device_id={"lat": to_lat, "tp": to_core},
            device_id_type=pl.DeviceIdType.MESH,
        )

    mine = part_ref[0].astype(f32)
    quarters = [mine[:, q * quarter:(q + 1) * quarter] for q in range(4)]
    for k in range(2):
        part[k] = jnp.concatenate([v[4 * k:4 * k + 4] for v in quarters], axis=0).astype(bf16)

    keep_row = (ids_ref[...] >= 3).astype(f32)

    def keep_column(rows, token_of):
        at = lax.broadcasted_iota(jnp.int32, (rows, tokens), 1)
        row = lax.broadcasted_iota(jnp.int32, (rows, tokens), 0)
        return jnp.sum(jnp.where(at == token_of(row), keep_row, 0.0), axis=1, keepdims=True)

    keep = keep_column(tokens, lambda i: (((i // 8) % far) * NEAR + (i // 8) // far) * 8 + i % 8)
    keep_mine = keep_column(16, lambda i: lat * 8 + core * 4 + i % 4)

    pl.semaphore_wait(barrier, len(peers))

    def gather(turn, ref, beside=None):
        mine_at = ref.at[core, b, a]
        sent = [
            send(mine_at, mine_at, ag_far, (turn, k), fars(k, 1) * NEAR + b, core)
            for k in range(1, far)
        ]
        near_copies, core_copies = [], []
        for k in range(far):
            origin = fars(k, -1)
            if k > 0:
                sent[k - 1].wait_recv()
            block = ref.at[core, b, origin]
            near_copies.append(send(block, block, ag_near, (turn, k), a * NEAR + nb, core))
            core_copies.append(send(block, block, ag_core, (turn, k), lat, other))
        if beside is not None:
            beside()
        for k in range(far):
            near_copies[k].wait_recv()
            block = ref.at[core, nb, fars(k, -1)]
            core_copies.append(send(block, block, ag_core, (turn, far + k), lat, other))
        for copy in core_copies:
            copy.wait_recv()
        for copy in sent + near_copies + core_copies:
            copy.wait_send()

    def unpack(ref, out):
        halves = [ref[k].astype(f32).reshape(NEAR * far, 16, quarter) for k in range(2)]
        for q in range(4):
            out[q] = (
                jnp.concatenate([v[:, 4 * q:4 * q + 4, :] for v in halves], axis=1)
                .reshape(tokens, quarter)
                .astype(bf16)
            )

    def scatter(turn, left, weight, beside):
        pieces = [
            jnp.dot(
                left, weight[:, q * quarter:(q + 1) * quarter], preferred_element_type=f32
            ).reshape(NEAR * far, 8, quarter)
            for q in range(4)
        ]
        for k in range(2):
            rows = jnp.concatenate([v[:, 4 * k:4 * k + 4, :] for v in pieces], axis=1)
            outgoing[k] = rows.astype(bf16).reshape(NEAR, far, 16, quarter)
        first = [
            send(outgoing.at[other, side], pair_in.at[turn, side], rs_core, (turn, i), lat, other)
            for i, side in enumerate((nb, b))
        ]
        first[0].wait_recv()
        near_copies = []
        for k in [*range(1, far), 0]:
            to = fars(k, 1)
            near_out[to] = (
                outgoing[core, nb, to].astype(f32) + pair_in[turn, nb, to].astype(f32)
            ).astype(bf16)
            near_copies.append(
                send(near_out.at[to], near_in.at[turn, to], rs_near, (turn, k), a * NEAR + nb, core)
            )
        beside[0]()
        first[1].wait_recv()
        far_copies = []
        for k in [*range(1, far), 0]:
            to = fars(k, 1)
            near_copies[k - 1 if k > 0 else far - 1].wait_recv()
            summed = (
                outgoing[core, b, to].astype(f32)
                + pair_in[turn, b, to].astype(f32)
                + near_in[turn, to].astype(f32)
            )
            if k > 0:
                far_out[k] = summed.astype(bf16)
                far_copies.append(
                    send(far_out.at[k], far_in.at[turn, k], rs_far, (turn, k), to * NEAR + b, core)
                )
        beside[1]()
        for k in range(1, far):
            far_copies[k - 1].wait_recv()
            summed = summed + far_in[turn, k].astype(f32)
        for copy in first + near_copies + far_copies:
            copy.wait_send()
        return summed

    pair = send(part.at[other], part_in, pair_sems, (), lat, other)
    pair.wait_recv()
    acts_all[core, b, a] = (part[core].astype(f32) + part_in[...].astype(f32)).astype(bf16)
    gather(0, acts_all, loads[0].wait)
    pair.wait_send()
    unpack(acts_all, acts)

    def against(matrix, weight):
        total = None
        for q in range(4):
            term = lax.dot_general(
                matrix[q], weight[:, q * quarter:(q + 1) * quarter],
                (((1,), (1,)), ((), ())), preferred_element_type=f32,
            )
            total = term if total is None else total + term
        return total

    both = bias_ref[...].reshape(1, -1)
    bias = jnp.where(core == 0, both[:, :lats], both[:, lats:])
    eight = 8.0 * (against(acts, enc) + bias)
    small = jnp.exp(-jnp.abs(eight))
    act = ((jnp.maximum(eight, 0.0) + jnp.log1p(small)) / 8.0).astype(bf16)
    slope = jnp.where(eight >= 0, 1.0, small) / (1.0 + small)

    def nothing():
        pass

    loads[1].wait()
    total = scatter(0, act, dec, (nothing, nothing))
    signal_mine = (keep_mine * (total - acts_all[core, b, a].astype(f32))).astype(bf16)
    signal_all[core, b, a] = signal_mine

    def write_recon():
        for q in range(4):
            recon_ref[:, q * quarter:(q + 1) * quarter] = total[4 * q:4 * q + 4].astype(bf16)

    gather(1, signal_all, write_recon)
    unpack(signal_all, signal)

    back = against(signal, dec) + L1_WEIGHT * keep
    dpre = (back * slope).astype(bf16)
    act_ref[...] = act
    dpre_ref[...] = dpre

    def store(matrix, hbm, index):
        copy = pltpu.make_async_copy(matrix, hbm, store_sem.at[index])
        copy.start()
        return copy

    stores = [store(acts, acts_hbm, 0), store(signal, signal_hbm, 1)]
    inward = scatter(1, dpre, enc, (nothing, nothing))
    inward = inward - signal_mine.astype(f32)
    for q in range(4):
        igrad_ref[:, q * quarter:(q + 1) * quarter] = inward[4 * q:4 * q + 4]
    for copy in stores:
        copy.wait()


def gradients(
    acts, signal, act, dpre, recon_in, igrad_in, recon, igrad, genc, gdec, gbias
):
    for left, right, out in ((dpre, acts, genc), (act, signal, gdec)):
        out[...] = lax.dot_general(
            left[...], right[0], (((0,), (0,)), ((), ())), preferred_element_type=f32
        ).astype(bf16)

    @pl.when(pl.program_id(0) == 0)
    def _():
        recon[...] = recon_in[...]
        igrad[...] = igrad_in[...]
        gbias[...] = jnp.sum(dpre[...].astype(f32), axis=0, keepdims=True)


def on_device(partials, token_ids, enc_weight, enc_bias, dec_weight):
    n_lat = lax.axis_size("lat")
    far = n_lat // NEAR
    tokens = token_ids.shape[0]
    width = enc_weight.shape[1]
    lats = enc_weight.shape[0] // 2
    quarter = width // 4
    vmem = pl.BlockSpec(memory_space=pltpu.VMEM)
    hbm = pl.BlockSpec(memory_space=pl.ANY)
    dma = pltpu.SemaphoreType.DMA
    flops = 2 * 6 * tokens * lats * width
    recon, igrad, acts, signal, act, dpre = pl.pallas_call(
        functools.partial(kernel, far, tokens, lats, width),
        out_shape=(
            jax.ShapeDtypeStruct((4, width), bf16),
            jax.ShapeDtypeStruct((4, width), f32),
            jax.ShapeDtypeStruct((4, tokens, quarter), bf16),
            jax.ShapeDtypeStruct((4, tokens, quarter), bf16),
            jax.ShapeDtypeStruct((tokens, lats), bf16),
            jax.ShapeDtypeStruct((tokens, lats), bf16),
        ),
        in_specs=[vmem, vmem, hbm, vmem, hbm],
        out_specs=(vmem, vmem, hbm, hbm, vmem, vmem),
        scratch_shapes=[
            pltpu.VMEM((lats, width), bf16),
            pltpu.VMEM((lats, width), bf16),
            pltpu.VMEM((2, 16, quarter), bf16),
            pltpu.VMEM((16, quarter), bf16),
            pltpu.VMEM((2, NEAR, far, 16, quarter), bf16),
            pltpu.VMEM((2, NEAR, far, 16, quarter), bf16),
            pltpu.VMEM((4, tokens, quarter), bf16),
            pltpu.VMEM((4, tokens, quarter), bf16),
            pltpu.VMEM((2, NEAR, far, 16, quarter), bf16),
            pltpu.VMEM((2, NEAR, far, 16, quarter), bf16),
            pltpu.VMEM((far, 16, quarter), bf16),
            pltpu.VMEM((2, far, 16, quarter), bf16),
            pltpu.VMEM((far, 16, quarter), bf16),
            pltpu.VMEM((2, far, 16, quarter), bf16),
            dma((2,)),
            dma((2,)),
            dma((2,)),
            dma((2, 2, far)),
            dma((2, 2, far)),
            dma((2, 2, 2 * far)),
            dma((2, 2, 2)),
            dma((2, 2, far)),
            dma((2, 2, far)),
        ],
        compiler_params=pltpu.CompilerParams(
            collective_id=0, has_side_effects=True, vmem_limit_bytes=60 * 2**20
        ),
        cost_estimate=pl.CostEstimate(
            flops=flops, bytes_accessed=8 * lats * width, transcendentals=4 * tokens * lats
        ),
    )(partials, token_ids.reshape(1, -1), enc_weight, enc_bias, dec_weight)

    def whole(*shape):
        return pl.BlockSpec(shape, lambda i: (0,) * len(shape))

    by_tokens = pl.BlockSpec((1, tokens, quarter), lambda i: (i, 0, 0))
    by_lats = pl.BlockSpec((lats, quarter), lambda i: (0, i))
    recon, igrad, genc, gdec, gbias = pl.pallas_call(
        gradients,
        grid=(4,),
        out_shape=(
            jax.ShapeDtypeStruct((4, width), bf16),
            jax.ShapeDtypeStruct((4, width), f32),
            jax.ShapeDtypeStruct((lats, width), bf16),
            jax.ShapeDtypeStruct((lats, width), bf16),
            jax.ShapeDtypeStruct((1, lats), f32),
        ),
        in_specs=[
            by_tokens, by_tokens, whole(tokens, lats), whole(tokens, lats),
            whole(4, width), whole(4, width),
        ],
        out_specs=(whole(4, width), whole(4, width), by_lats, by_lats, whole(1, lats)),
        compiler_params=pltpu.CompilerParams(vmem_limit_bytes=60 * 2**20),
        cost_estimate=pl.CostEstimate(
            flops=4 * tokens * lats * width,
            bytes_accessed=4 * (lats + tokens) * width,
            transcendentals=0,
        ),
    )(acts, signal, act, dpre, recon, igrad)
    return recon, igrad, genc, gdec, gbias.reshape(-1)


def solution(mesh):
    placed = (
        P("tp", ("groups", "lat"), None),
        P("groups"),
        P("lat", None),
        P("lat"),
        P("lat", None),
    )
    split = P(("groups", "lat", "tp"), None)
    return jax.shard_map(
        on_device,
        mesh=mesh,
        in_specs=placed,
        out_specs=(split, split, split, split, P(("groups", "lat", "tp"))),
        check_vma=False,
    )
```
